32 devices in a mesh: row: 4 (over y, x), col: 8 (over z, core).
Axes of the slice: x: 2, y: 2, z: 4, core: 2. Of those that a mesh axis runs over, the one named last changes fastest.
Arguments:
- factor_blocks: bfloat16 [6, 8, 1024, 4, 2048], P(None, None, 'row', None, 'col'), may hold values from -0.03125 to 0.03125
- inverse_blocks: bfloat16 [4, 4, 2048, 8, 1024], P(None, None, 'col', None, 'row'), as said below
- right_side: bfloat16 [4, 8, 1024, 128], P(None, None, 'row'), may hold values from -4 to 4
- centers: bfloat16 [16, 2048, 512], P(None, 'col')
- owner_map: int32 [16, 8], P(None, 'col'), may hold values from 0 to 15, as said below
- test_pool: bfloat16 [24576, 512], P('row')
- test_rows: int32 [16384], P('row'), may hold values from 0 to 24575, as said below
Outputs:
- coefficients: float32 [4, 4, 2048, 128], P(None, None, 'col')
- predictions: float32 [16384, 128], P(('row', 'col'))
The draws below stay inside these ranges and needn't reach their ends.
Inputs may be any that keep to these rules, and one draw needn't show every extreme that they name: `owner_map`: each column c is a permutation of 0 to 15. `test_rows`: entry i names a row of block i // 4096 of the pool, that is from (i // 4096) * 6144 to (i // 4096 + 1) * 6144 - 1; rows may repeat. `inverse_blocks`: read as D_k, each block is upper triangular with a positive diagonal.
All inputs are finite; a program needn't handle non-finite values.
Results may differ from the reference program's by a relative error of at most 0.019.
Values may be sent and summed in bfloat16 or wider, within the bound.
No kernel may reach another device: no remote copies, remote signals or barrier semaphores. Data moves between devices by JAX's collectives and lax.ppermute only.
A program may use at most 192 MiB of HBM per device.

```python
import jax
import jax.numpy as jnp
from jax import lax

PANEL = 8192
TILE = 256
NP = 4
DIM = 512
OUT = 128
TEST_DEV = 4096
TPP = 32
RT = 8
CT = 4
NLOC = 16
PAIRS = 6
POOL_DEV = 6144
POOL = 24576
NTEST = 16384
N_ROW = 4
N_COL = 8


def point_cloud(key, amount):
    feature = jnp.arange(DIM, dtype=jnp.float32)
    spread = 1.0 / jnp.sqrt(feature + 1.0)
    values = jax.random.normal(key, (amount, DIM), jnp.float32) * spread[None, :]
    return values


def draw_centers(key, part):
    values = point_cloud(jax.random.fold_in(key, 11), NP * PANEL)
    return values.reshape(NLOC, NP * PANEL // NLOC, DIM).astype(jnp.bfloat16)


def draw_test_pool(key, part):
    return point_cloud(jax.random.fold_in(key, 13), POOL).astype(jnp.bfloat16)


def draw_inverse_blocks(key, part):
    col_count = TPP // CT
    row_count = TPP // RT
    left_iota = lax.broadcasted_iota(jnp.int32, (1, CT, col_count * TILE, 1, 1), 1)
    left_pos = lax.broadcasted_iota(jnp.int32, (1, CT, col_count * TILE, 1, 1), 2)
    right_iota = lax.broadcasted_iota(jnp.int32, (1, 1, 1, RT, row_count * TILE), 3)
    right_pos = lax.broadcasted_iota(jnp.int32, (1, 1, 1, RT, row_count * TILE), 4)
    left_index = (left_iota * col_count + left_pos // TILE) * TILE + left_pos % TILE
    right_index = (right_iota * row_count + right_pos // TILE) * TILE + right_pos % TILE
    layout = (NP, CT, col_count * TILE, RT, row_count * TILE)
    noise = jax.random.normal(key, layout, jnp.float32)
    upper = noise / jnp.sqrt(jnp.float32(PANEL))
    diagonal = jnp.exp(jax.random.uniform(jax.random.fold_in(key, 5), (NP, CT, col_count * TILE, 1, 1), jnp.float32, -0.6931472, 0.6931472))
    values = jnp.where(right_index > left_index, upper, jnp.where(right_index == left_index, diagonal, 0.0))
    return values.astype(jnp.bfloat16)


def single_permutation(subkey):
    return jax.random.permutation(subkey, NLOC)


def draw_owner_map(key, part):
    col_count = TPP // CT
    subkeys = jax.random.split(jax.random.fold_in(key, 17), col_count)
    orders = jax.vmap(single_permutation)(subkeys)
    return orders.T.astype(jnp.int32)


def draw_test_rows(key, part):
    groups = NTEST // TEST_DEV
    picks = jax.random.randint(jax.random.fold_in(key, 19), (groups, TEST_DEV), 0, POOL_DEV)
    picks = picks.at[:, 0].set(0).at[:, 1].set(POOL_DEV - 1)
    offsets = jnp.arange(groups, dtype=jnp.int32)[:, None] * POOL_DEV
    return (picks + offsets).reshape(NTEST).astype(jnp.int32)


def shard_levels(stream_key, shape, pieces, low, high):
    def one(position, shards_of):
        draws = jax.random.uniform(jax.random.fold_in(jax.random.fold_in(stream_key, 6), position), (shards_of,), jnp.float32, low / len(pieces), high / len(pieces))
        return jnp.repeat(jnp.exp(draws), shape[position] // shards_of).reshape((-1,) + (1,) * (len(shape) - position - 1))

    gain = one(*pieces[0])
    for cut in pieces[1:]:
        gain = gain * one(*cut)
    return gain


def bell_draw(key, shape, scale, limit, cuts=(), kind=jnp.bfloat16):
    values = jax.random.normal(key, shape, jnp.float32) * scale
    if len(cuts) > 0:
        values = shard_levels(key, shape, cuts, -0.22, 0.18) * values
    return jnp.clip(values, min=-limit, max=limit).astype(kind)


def setup_inputs(seed: int = 0) -> dict:
    key_of = jax.random.split(jax.random.key(seed), 8)
    factor_blocks = bell_draw(key_of[0], (PAIRS, RT, N_ROW * TILE, CT, N_COL * TILE), (4 * PANEL) ** -0.5, 0.03125, ((2, 4), (4, 8)))
    inverse_blocks = draw_inverse_blocks(jax.random.fold_in(key_of[7], 71), 0)
    right_side = bell_draw(key_of[2], (NP, RT, N_ROW * TILE, OUT), 0.25, 4.0, ((2, 4),))
    centers = draw_centers(jax.random.fold_in(key_of[7], 71), 0)
    owner_map = draw_owner_map(jax.random.fold_in(key_of[7], 71), 0)
    test_pool = draw_test_pool(jax.random.fold_in(key_of[7], 71), 0)
    test_rows = draw_test_rows(jax.random.fold_in(key_of[7], 71), 0)
    return dict(factor_blocks=factor_blocks, inverse_blocks=inverse_blocks, right_side=right_side, centers=centers, owner_map=owner_map, test_pool=test_pool, test_rows=test_rows)


inverse_width = 0.35


def pair_slot(early, successor):
    return successor * (successor - 1) // 2 + early


def reference(factor_blocks, inverse_blocks, right_side, centers, owner_map, test_pool, test_rows):
    pair_blocks = factor_blocks.reshape(PAIRS, PANEL, PANEL)
    inverse = inverse_blocks.reshape(NP, PANEL, PANEL)
    targets = right_side.reshape(NP, PANEL, OUT).astype(jnp.float32)
    solved = [None] * NP
    rounded = [None] * NP
    for current in range(NP - 1, -1, -1):
        summed = jnp.zeros((PANEL, OUT), jnp.float32)
        for successor in range(current + 1, NP):
            summed = summed + jnp.dot(pair_blocks[pair_slot(current, successor)], rounded[successor], preferred_element_type=jnp.float32)
        residue = (targets[current] - summed).astype(jnp.bfloat16)
        solved[current] = jnp.dot(inverse[current], residue, preferred_element_type=jnp.float32)
        rounded[current] = solved[current].astype(jnp.bfloat16)
    coefficient = jnp.stack(rounded).reshape(NLOC, N_COL, TILE, OUT)
    picks = jnp.broadcast_to(owner_map[:, :, None, None], (NLOC, N_COL, TILE, OUT))
    paired = jnp.take_along_axis(coefficient, picks, axis=0).reshape(NLOC * N_COL * TILE, OUT)
    span_rows = jnp.take(test_pool, test_rows, axis=0)
    flat_centers = centers.reshape(NLOC * N_COL * TILE, DIM)
    center_sq = jnp.sum(jnp.square(flat_centers.astype(jnp.float32)), axis=1)
    height = min(512, NTEST)

    def scoring(block_rows):
        block_sq = jnp.sum(jnp.square(block_rows.astype(jnp.float32)), axis=1)
        crossed = jnp.dot(block_rows, flat_centers.T, preferred_element_type=jnp.float32)
        distance = block_sq[:, None] + center_sq[None, :] - 2.0 * crossed
        kernel = jnp.exp(-inverse_width * distance).astype(jnp.bfloat16)
        return jnp.dot(kernel, paired, preferred_element_type=jnp.float32)

    estimate = lax.map(scoring, span_rows.reshape(NTEST // height, height, DIM)).reshape(NTEST, OUT)
    alpha = jnp.stack(solved).reshape(NP, CT, N_COL * TILE, OUT)
    return alpha, estimate
```

```python
import math

import jax
import jax.numpy as jnp
from jax import lax
from jax.experimental import pallas as pl
from jax.experimental.pallas import tpu as pltpu
from jax.sharding import PartitionSpec as P

inverse_width = 0.35
log2e = math.log2(math.e)
scale = -inverse_width * log2e
bf16 = jnp.bfloat16
f32 = jnp.float32
vmem = pl.BlockSpec(memory_space=pltpu.VMEM)
anywhere = pl.BlockSpec(memory_space=pl.ANY)


def params(mib=48):
    return pltpu.CompilerParams(vmem_limit_bytes=mib * 2**20)


def pair_slot(early, successor):
    return successor * (successor - 1) // 2 + early


def panel_product(blocks, slot, vector, earlier, out_dtype, name):
    _, groups, rows, inner, width = blocks.shape
    depth = inner * width
    out_width = vector.shape[1]

    def body(*refs):
        if earlier is None:
            block_ref, vector_ref, out_ref, held, sem = refs
        else:
            block_ref, vector_ref, earlier_ref, out_ref, held, sem = refs
        copies = [
            pltpu.make_async_copy(block_ref.at[slot, g], held.at[g], sem.at[g]) for g in range(groups)
        ]
        for copy in copies:
            copy.start()
        for g in range(groups):
            copies[g].wait()
            at = pl.ds(g * rows, rows)
            value = jnp.dot(
                held[g].reshape(rows, depth), vector_ref[...], preferred_element_type=f32
            )
            if earlier is not None:
                value = value + earlier_ref[at, :]
            out_ref[at, :] = value.astype(out_dtype)

    operands = [blocks, vector] + ([] if earlier is None else [earlier])
    return pl.pallas_call(
        body,
        in_specs=[anywhere] + [vmem] * (len(operands) - 1),
        out_specs=vmem,
        out_shape=jax.ShapeDtypeStruct((groups * rows, out_width), out_dtype),
        scratch_shapes=[
            pltpu.VMEM((groups, rows, inner, width), bf16),
            pltpu.SemaphoreType.DMA((groups,)),
        ],
        compiler_params=params(),
        cost_estimate=pl.CostEstimate(
            flops=4 * groups * rows * depth * out_width,
            bytes_accessed=2 * groups * rows * depth,
            transcendentals=0,
        ),
        name=name,
    )(*operands)


def kernel_values(span, center, center_sq, test_sq):
    crossed = lax.dot_general(
        span, center, (((1,), (1,)), ((), ())), preferred_element_type=f32
    )
    reps = center.shape[0] // test_sq.shape[1]
    test_part = jnp.concatenate([test_sq] * reps, axis=1)
    return jnp.exp2((crossed * (-2.0 * scale) + center_sq) + test_part).astype(bf16)


def kernel_block(span, centers, center_sq, slots, name):
    tests, dim = span.shape
    tiles = slots.shape[0]
    size = centers.shape[1]
    step = min(512, tests)

    def body(slots_ref, span_ref, *refs):
        center_refs, sq_refs = refs[:tiles], refs[tiles : 2 * tiles]
        out_ref, norm_ref = refs[2 * tiles :]
        rows = span_ref[...]
        wide = rows.astype(f32)
        norm = scale * jnp.sum(wide * wide, axis=1, keepdims=True)
        norm = jnp.broadcast_to(norm, norm_ref.shape)
        norm_ref[...] = norm
        for t in range(tiles):
            out_ref[:, t * size : (t + 1) * size] = kernel_values(
                rows, center_refs[t][0], sq_refs[t][0], norm
            )

    center_specs = [
        pl.BlockSpec((1, size, dim), lambda i, s, t=t: (s[t], 0, 0)) for t in range(tiles)
    ]
    sq_specs = [pl.BlockSpec((1, 1, size), lambda i, s, t=t: (s[t], 0, 0)) for t in range(tiles)]
    return pl.pallas_call(
        body,
        grid_spec=pltpu.PrefetchScalarGridSpec(
            num_scalar_prefetch=1,
            grid=(tests // step,),
            in_specs=[pl.BlockSpec((step, dim), lambda i, s: (i, 0))] + center_specs + sq_specs,
            out_specs=[
                pl.BlockSpec((step, tiles * size), lambda i, s: (i, 0)),
                pl.BlockSpec((step, 128), lambda i, s: (i, 0)),
            ],
        ),
        out_shape=[
            jax.ShapeDtypeStruct((tests, tiles * size), bf16),
            jax.ShapeDtypeStruct((tests, 128), f32),
        ],
        compiler_params=params(),
        cost_estimate=pl.CostEstimate(
            flops=3 * tests * tiles * size * dim,
            bytes_accessed=2 * tests * tiles * size,
            transcendentals=tests * tiles * size,
        ),
        name=name,
    )(slots, span, *([centers] * tiles), *([center_sq] * tiles))


def scored_block(span, norms, centers, center_sq, slots, weights, earlier, name):
    tests, dim = span.shape
    tiles = slots.shape[0]
    size = centers.shape[1]
    width = weights.shape[1]
    step = min(512, tests)
    more = 0 if earlier is None else 1

    def body(slots_ref, span_ref, norm_ref, weight_ref, *refs):
        center_refs, sq_refs = refs[:tiles], refs[tiles : 2 * tiles]
        out_ref = refs[-1]
        rows = span_ref[...]
        norm = norm_ref[...]
        total = refs[2 * tiles][...] if more else None
        for t in range(tiles):
            values = kernel_values(rows, center_refs[t][0], sq_refs[t][0], norm)
            part = jnp.dot(
                values, weight_ref[t * size : (t + 1) * size, :], preferred_element_type=f32
            )
            total = part if total is None else total + part
        out_ref[...] = total

    center_specs = [
        pl.BlockSpec((1, size, dim), lambda i, s, t=t: (s[t], 0, 0)) for t in range(tiles)
    ]
    sq_specs = [pl.BlockSpec((1, 1, size), lambda i, s, t=t: (s[t], 0, 0)) for t in range(tiles)]
    row_spec = pl.BlockSpec((step, width), lambda i, s: (i, 0))
    return pl.pallas_call(
        body,
        grid_spec=pltpu.PrefetchScalarGridSpec(
            num_scalar_prefetch=1,
            grid=(tests // step,),
            in_specs=[
                pl.BlockSpec((step, dim), lambda i, s: (i, 0)),
                pl.BlockSpec((step, 128), lambda i, s: (i, 0)),
                pl.BlockSpec(weights.shape, lambda i, s: (0, 0)),
            ]
            + center_specs
            + sq_specs
            + [row_spec] * more,
            out_specs=row_spec,
        ),
        out_shape=jax.ShapeDtypeStruct((tests, width), f32),
        compiler_params=params(),
        cost_estimate=pl.CostEstimate(
            flops=3 * tests * tiles * size * (dim + 2 * width),
            bytes_accessed=2 * (tests + tiles * size) * dim,
            transcendentals=tests * tiles * size,
        ),
        name=name,
    )(
        slots, span, norms, weights, *([centers] * tiles), *([center_sq] * tiles),
        *([earlier] if more else []),
    )


def final_block(kernel, weights, earlier, name):
    tests, depth = kernel.shape
    width = weights.shape[1]
    step = min(1024, tests)

    def body(kernel_ref, weight_ref, earlier_ref, out_ref):
        value = jnp.dot(kernel_ref[...], weight_ref[...], preferred_element_type=f32)
        out_ref[...] = (value + earlier_ref[...]).astype(bf16)

    return pl.pallas_call(
        body,
        grid=(tests // step,),
        in_specs=[
            pl.BlockSpec((step, depth), lambda i: (i, 0)),
            pl.BlockSpec((depth, width), lambda i: (0, 0)),
            pl.BlockSpec((step, width), lambda i: (i, 0)),
        ],
        out_specs=pl.BlockSpec((step, width), lambda i: (i, 0)),
        out_shape=jax.ShapeDtypeStruct((tests, width), bf16),
        compiler_params=params(),
        cost_estimate=pl.CostEstimate(
            flops=4 * tests * depth * width, bytes_accessed=2 * tests * depth, transcendentals=0
        ),
        name=name,
    )(kernel, weights, earlier)


def swap(value, axis, mask):
    size = lax.axis_size(axis)
    return lax.ppermute(value, axis, [(i, i ^ mask) for i in range(size)])


def added(left, right):
    return left.astype(f32) + right.astype(f32)


def parted(value, pick):
    half = value.shape[0] // 2
    return (
        lax.dynamic_slice_in_dim(value, pick * half, half, 0),
        lax.dynamic_slice_in_dim(value, (1 - pick) * half, half, 0),
    )


def joined(mine, other, pick):
    first = jnp.where(pick == 0, mine, other)
    second = jnp.where(pick == 0, other, mine)
    return jnp.concatenate([first, second], axis=0)


def col_picks():
    size = lax.axis_size("col")
    bits = size.bit_length() - 1
    place = lax.axis_index("col")
    bit = [(place >> j) & 1 for j in range(bits)]
    picks = [(1 << j, bit[j]) for j in range(bits - 1)]
    last = 1 << (bits - 1)
    if bits >= 3:
        picks[-1] = (1 << (bits - 2), bit[bits - 2] ^ bit[bits - 1])
        last = last | (1 << (bits - 2))
    return picks, last


def row_sum(partial):
    bits = lax.axis_size("row").bit_length() - 1
    half = partial.shape[0] // 2
    parts = [partial[:half], partial[half:]]
    orders = [list(range(bits)), list(range(bits))[::-1]]
    for j in range(bits):
        received = [swap(p, "row", 1 << o[j]) for p, o in zip(parts, orders)]
        parts = [added(p, r) for p, r in zip(parts, received)]
        if j < bits - 1:
            parts = [p.astype(bf16) for p in parts]
    return jnp.concatenate(parts, axis=0)


def subtracted(targets, partial):
    picks, last = col_picks()
    total, own = partial, targets
    for mask, pick in picks:
        mine, other = parted(total, pick)
        total = added(mine, swap(other, "col", mask)).astype(bf16)
        own = parted(own, pick)[0]
    total = added(total, swap(total, "col", last))
    value = (own.astype(f32) - total).astype(bf16)
    for mask, pick in picks[::-1]:
        value = joined(value, swap(value, "col", mask), pick)
    return value


def scattered(partial):
    size = lax.axis_size("col")
    place = lax.axis_index("col")
    bits = size.bit_length() - 1
    height = partial.shape[0] // size
    total = partial.reshape((2,) * bits + (height, partial.shape[1]))
    total = total.transpose(tuple(range(bits))[::-1] + (bits, bits + 1))
    total = total.reshape(partial.shape)
    for j in range(bits):
        mine, other = parted(total, (place >> j) & 1)
        total = added(mine, swap(other, "col", 1 << j))
        if j < bits - 1:
            total = total.astype(bf16)
    return total


def shards(factor_blocks, inverse_blocks, right_side, centers, owner_map, test_pool, test_rows):
    panels = inverse_blocks.shape[0]
    col_tiles = inverse_blocks.shape[1]
    tile_size = inverse_blocks.shape[2]
    row_tiles = inverse_blocks.shape[3]
    width_out = right_side.shape[3]
    own_rows = row_tiles * tile_size
    targets = right_side.reshape(panels, own_rows, width_out)
    tests = test_rows.shape[0]
    chunks = 4
    chunk = tests // chunks

    slots = jnp.argsort(owner_map[:, 0]).astype(jnp.int32)
    located = test_rows - lax.axis_index("row") * test_pool.shape[0]
    span = [
        test_pool.at[located[i * chunk : (i + 1) * chunk]].get(mode="promise_in_bounds")
        for i in range(chunks)
    ]
    center_sq = scale * jnp.sum(jnp.square(centers.astype(f32)), axis=2)
    center_sq = center_sq[:, None, :]

    def panel_slots(k):
        return slots[k * col_tiles : (k + 1) * col_tiles]

    first = [
        kernel_block(span[i], centers, center_sq, panel_slots(0), f"kernel_0_{i}")
        for i in range(chunks)
    ]
    totals = [None] * chunks
    solved = [None] * panels
    rounded = [None] * panels
    partial = [None] * panels
    for k in range(panels - 1, -1, -1):
        if k == panels - 1:
            residue = targets[k]
        else:
            residue = subtracted(targets[k], partial[k])
        product = panel_product(inverse_blocks, k, residue, None, bf16, f"inverse_{k}")
        solved[k] = row_sum(product)
        rounded[k] = solved[k].astype(bf16)
        for early in range(k - 1, -1, -1):
            partial[early] = panel_product(
                factor_blocks,
                pair_slot(early, k),
                rounded[k],
                partial[early],
                bf16 if early == k - 1 else f32,
                f"factor_{early}_{k}",
            )
        if k > 0:
            totals = [
                scored_block(
                    span[i], first[i][1], centers, center_sq, panel_slots(k), rounded[k], totals[i],
                    f"scored_{k}_{i}",
                )
                for i in range(chunks)
            ]
    estimate = jnp.concatenate(
        [final_block(first[i][0], rounded[0], totals[i], f"final_{i}") for i in range(chunks)], axis=0
    )
    estimate = scattered(estimate)
    alpha = jnp.stack(solved).reshape(panels, col_tiles, tile_size, width_out)
    return (alpha, estimate)


def solution(mesh):
    in_specs = (
        P(None, None, "row", None, "col"),
        P(None, None, "col", None, "row"),
        P(None, None, "row", None),
        P(None, "col", None),
        P(None, "col"),
        P("row", None),
        P("row"),
    )
    out_specs = (P(None, None, "col", None), P(("row", "col"), None))
    return jax.shard_map(shards, mesh=mesh, in_specs=in_specs, out_specs=out_specs, check_vma=False)
```

```python
import math

import jax
import jax.numpy as jnp
import numpy as np
from jax import lax
from jax.experimental import pallas as pl
from jax.experimental.pallas import tpu as pltpu
from jax.sharding import PartitionSpec as P

inverse_width = 0.35
log2e = math.log2(math.e)
scale = -inverse_width * log2e
row_room, core_room, near_room, far_room = 3.3, 1.2, 3.0, 5.5
row_parts = 2
flying = 8
bf16 = jnp.bfloat16
f32 = jnp.float32
vmem = pl.BlockSpec(memory_space=pltpu.VMEM)
smem = pl.BlockSpec(memory_space=pltpu.SMEM)
stays = pl.BlockSpec(memory_space=pltpu.HBM)


def params(mib):
    return pltpu.CompilerParams(vmem_limit_bytes=mib * 2**20)


def pair_slot(early, successor):
    return successor * (successor - 1) // 2 + early


def fetches(block_ref, slot, held, sem):
    return [
        pltpu.make_async_copy(block_ref.at[slot, g], held.at[g], sem.at[g])
        for g in range(held.shape[0])
    ]


def panel_product(blocks, slot, kept, vector, vector_flip, earlier, out_parts, out_flip, out_dtype, name):
    _, groups, rows, inner, width = blocks.shape
    depth = inner * width
    out_width = vector.shape[-1]
    in_parts = vector.shape[0]
    part_rows = groups * rows // out_parts
    unit = min(rows, part_rows)
    flips = [f for f in (vector_flip, out_flip) if f is not None]
    more = [] if earlier is None else [earlier]

    def body(*refs):
        flip_refs, refs = list(refs[: len(flips)]), refs[len(flips) :]
        block_ref, vector_ref = refs[:2]
        out_ref = refs[2 + len(more)]
        held, sem = refs[3 + len(more) :] if kept is None else (block_ref, None)
        in_flip = 0 if vector_flip is None else flip_refs.pop(0)[0]
        flip = 0 if out_flip is None else flip_refs.pop(0)[0]
        copies = []
        if kept is None:
            copies = fetches(block_ref, slot, held, sem)
        for copy in copies[:flying]:
            copy.start()
        if in_parts == 1:
            column = vector_ref[0]
        elif vector_flip is None:
            column = vector_ref[...].reshape(depth, out_width)
        else:
            column = jnp.concatenate([vector_ref[p ^ in_flip] for p in range(in_parts)], axis=0)
        for g in range(groups):
            if kept is None:
                copies[g].wait()
                for copy in copies[g + flying : g + flying + 1]:
                    copy.start()
            for u in range(rows // unit):
                part, at = divmod(g * rows + u * unit, part_rows)
                at = pl.ds(at, unit)
                value = jnp.dot(
                    held[g, u * unit : (u + 1) * unit].reshape(unit, depth),
                    column,
                    preferred_element_type=f32,
                )
                if more:
                    value = value + refs[2][part ^ flip, at, :]
                out_ref[part ^ flip, at, :] = value.astype(out_dtype)

    source = pltpu.with_memory_space_constraint(blocks, pltpu.HBM) if kept is None else kept
    return pl.pallas_call(
        body,
        in_specs=[smem] * len(flips) + [stays if kept is None else vmem] + [vmem] * (1 + len(more)),
        out_specs=vmem,
        out_shape=jax.ShapeDtypeStruct((out_parts, part_rows, out_width), out_dtype),
        scratch_shapes=[
            pltpu.VMEM((groups, rows, inner, width), bf16),
            pltpu.SemaphoreType.DMA((groups,)),
        ]
        if kept is None
        else [],
        compiler_params=params(8),
        cost_estimate=pl.CostEstimate(
            flops=4 * groups * rows * depth * out_width,
            bytes_accessed=2 * groups * rows * depth,
            transcendentals=0,
        ),
        name=name,
    )(*flips, source, vector, *more)


def gathered(located, pool, chunks, name):
    count = located.shape[0]
    rows, dim = pool.shape
    cuts = dim // 128
    chunk = count // chunks
    group = 64
    step = 128
    block = min(1024, rows)
    stages = min(6, rows // block)

    def body(located_ref, pool_ref, *refs):
        out_refs, norm_refs = refs[:chunks], refs[chunks : 2 * chunks]
        wide, held, staged, sem, rows_out, norms_out, out_sem = refs[2 * chunks :]
        copies = [
            pltpu.make_async_copy(
                pool_ref.at[pl.ds(b * block, block)], staged.at[b % stages], sem.at[b % stages]
            )
            for b in range(rows // block)
        ]

        def widen(b):
            def convert(i, carry):
                at = pl.multiple_of(i * step, step)
                value = staged[b % stages, pl.ds(at, step), :].astype(f32)
                for h in range(cuts):
                    to = pl.ds((b * block + at) * cuts + h, step, stride=cuts)
                    wide[to, :] = value[:, h * 128 : (h + 1) * 128]
                return carry

            lax.fori_loop(0, block // step, convert, 0)

        def part(j):
            def fetch(i, carry):
                for u in range(group):
                    at = i * group + u
                    source = pl.multiple_of(located_ref[j * chunk + at] * cuts, cuts)
                    held[pl.ds(pl.multiple_of(at * cuts, cuts), cuts), :] = wide[pl.ds(source, cuts), :]
                return carry

            def store(i, carry):
                at = pl.multiple_of(i * step, step)
                parts = [held[pl.ds(at * cuts + h, step, stride=cuts), :] for h in range(cuts)]
                rows_out[j % 2, pl.ds(at, step), :] = jnp.concatenate(parts, axis=1).astype(bf16)
                total = sum(p * p for p in parts)
                norm = scale * jnp.sum(total, axis=1, keepdims=True)
                norms_out[j % 2, pl.ds(at, step), :] = jnp.broadcast_to(norm, (step, 128))
                return carry

            lax.fori_loop(0, chunk // group, fetch, 0)
            lax.fori_loop(0, chunk // step, store, 0)

        for copy in copies[:stages]:
            copy.start()
        for b in range(len(copies)):
            copies[b].wait()
            widen(b)
            for copy in copies[b + stages : b + stages + 1]:
                copy.start()
        writes = []
        for j in range(chunks):
            for copy in writes[2 * (j - 2) : 2 * (j - 1)] if j >= 2 else []:
                copy.wait()
            part(j)
            for n, (source, to) in enumerate(((rows_out, out_refs), (norms_out, norm_refs))):
                writes.append(pltpu.make_async_copy(source.at[j % 2], to[j], out_sem.at[j % 2, n]))
                writes[-1].start()
        for copy in writes[2 * max(chunks - 2, 0) :]:
            copy.wait()

    return pl.pallas_call(
        body,
        in_specs=[smem, stays],
        out_specs=[stays] * (2 * chunks),
        out_shape=[pltpu.HBM((chunk, dim), bf16)] * chunks + [pltpu.HBM((chunk, 128), f32)] * chunks,
        scratch_shapes=[
            pltpu.VMEM((rows * cuts, 128), f32),
            pltpu.VMEM((chunk * cuts, 128), f32),
            pltpu.VMEM((stages, block, dim), bf16),
            pltpu.SemaphoreType.DMA((stages,)),
            pltpu.VMEM((2, chunk, dim), bf16),
            pltpu.VMEM((2, chunk, 128), f32),
            pltpu.SemaphoreType.DMA((2, 2)),
        ],
        compiler_params=params(28),
        cost_estimate=pl.CostEstimate(
            flops=0, bytes_accessed=6 * rows * dim + 16 * count * dim, transcendentals=0
        ),
        name=name,
    )(located, pltpu.with_memory_space_constraint(pool, pltpu.HBM))


def scored(span, norms, centers, center_sq, slots, weights, earlier, fetch, name):
    tests, dim = span.shape
    tiles = slots.shape[0]
    size = centers.shape[1]
    step = min(512 if weights is not None else 256, tests)
    steps = tests // step
    depth = tiles * size
    more = [x for x in (weights, earlier) if x is not None]
    fresh = center_sq is None

    def body(slots_ref, span_ref, norm_ref, center_ref, *refs):
        refs = list(refs)
        sq_ref = None if fresh else refs.pop(0)
        more_refs = [refs.pop(0) for _ in more]
        source = None if fetch is None else refs.pop(0)
        out_ref = refs.pop(0)
        if fresh:
            sq_ref = refs.pop(0)
        copies = []
        if fetch is not None:
            copies = fetches(source, fetch[1], refs.pop(0), refs.pop())
            for copy in copies:
                copy.start()
        if fresh:
            for t in range(tiles):
                value = center_ref[slots_ref[t]].astype(f32)
                sq_ref[t] = scale * jnp.sum(value * value, axis=1, keepdims=True).T
        writes = []
        if weights is None:
            values, sem = refs
            writes = [
                pltpu.make_async_copy(values.at[i], out_ref.at[pl.ds(i * step, step)], sem.at[i])
                for i in range(steps)
            ]
        for i in range(steps):
            at = slice(i * step, (i + 1) * step)
            rows = span_ref[at, :]
            norm = jnp.concatenate([norm_ref[at, :]] * (size // 128), axis=1)
            total = None if earlier is None else more_refs[1][at, :]
            for t in range(tiles):
                slot = slots_ref[t]
                crossed = lax.dot_general(
                    rows, center_ref[slot], (((1,), (1,)), ((), ())), preferred_element_type=f32
                )
                value = jnp.exp2((crossed * (-2.0 * scale) + sq_ref[t]) + norm).astype(bf16)
                place = slice(t * size, (t + 1) * size)
                if weights is None:
                    values[i, :, place] = value
                else:
                    part = jnp.dot(value, more_refs[0][place, :], preferred_element_type=f32)
                    total = part if total is None else total + part
            if weights is None:
                writes[i].start()
            else:
                out_ref[at, :] = total
        for copy in writes + copies:
            copy.wait()

    if weights is None:
        out_shapes, out_specs = [jax.ShapeDtypeStruct((tests, depth), bf16)], [stays]
        scratch = [pltpu.VMEM((steps, step, depth), bf16), pltpu.SemaphoreType.DMA((steps,))]
    else:
        out_shapes, out_specs = [jax.ShapeDtypeStruct((tests, weights.shape[1]), f32)], [vmem]
        scratch = []
    operands = [slots, span, norms, centers] + ([] if fresh else [center_sq]) + more
    in_specs = [smem] + [vmem] * (len(operands) - 1)
    if fresh:
        out_shapes = out_shapes + [jax.ShapeDtypeStruct((tiles, 1, size), f32)]
        out_specs = out_specs + [vmem]
    if fetch is not None:
        in_specs = in_specs + [stays]
        operands = operands + [pltpu.with_memory_space_constraint(fetch[0], pltpu.HBM)]
        out_shapes = out_shapes + [jax.ShapeDtypeStruct(fetch[0].shape[1:], fetch[0].dtype)]
        out_specs = out_specs + [vmem]
        scratch = scratch + [pltpu.SemaphoreType.DMA((fetch[0].shape[1],))]
    if weights is None:
        out_shapes[0] = pltpu.HBM(out_shapes[0].shape, out_shapes[0].dtype)
    made = pl.pallas_call(
        body,
        in_specs=in_specs,
        out_specs=out_specs,
        out_shape=out_shapes,
        scratch_shapes=scratch,
        compiler_params=params(8),
        cost_estimate=pl.CostEstimate(
            flops=3 * tests * depth * dim,
            bytes_accessed=2 * tests * dim,
            transcendentals=tests * depth,
        ),
        name=name,
    )(*operands)
    sq = made[1] if fresh else center_sq
    return made[0], sq, made[-1] if fetch is not None else None


def finished(kernels, weights, totals, places):
    blocks = places.shape[0]
    tests, depth = kernels[0].shape
    width = weights.shape[1]
    height = len(kernels) * tests // blocks
    unit = min(height, tests)

    def body(places_ref, *refs):
        kernel_refs, weight_ref = refs[: len(kernels)], refs[len(kernels)]
        total_refs, out_ref = refs[len(kernels) + 1 : -1], refs[-1]
        for start in range(0, blocks * height, unit):
            c, at = divmod(start, tests)
            block, within = divmod(start, height)
            value = jnp.dot(
                kernel_refs[c][at : at + unit, :], weight_ref[...], preferred_element_type=f32
            )
            value = value + total_refs[c][at : at + unit, :]
            out_ref[places_ref[block], within : within + unit, :] = value.astype(bf16)

    return pl.pallas_call(
        body,
        in_specs=[smem] + [vmem] * (len(kernels) + 1 + len(totals)),
        out_specs=vmem,
        out_shape=jax.ShapeDtypeStruct((blocks, height, width), bf16),
        compiler_params=params(8),
        cost_estimate=pl.CostEstimate(
            flops=4 * blocks * height * depth * width,
            bytes_accessed=2 * blocks * height * depth,
            transcendentals=0,
        ),
        name="finished",
    )(places, *kernels, weights, *totals)


class Piece:
    def __init__(self, cost, make, fetches=False):
        self.cost, self.make, self.done, self.fetches = cost, make, False, fetches

    def run(self, before, fetch=None):
        if not self.done:
            self.done = True
            return self.make(before, fetch) if fetch else self.make(before)


class Beside:
    def __init__(self):
        self.pieces = []
        self.wanted = None
        self.fetched = None

    def want(self, wanted):
        self.wanted, self.fetched = wanted, None

    def take(self):
        fetched, self.wanted, self.fetched = self.fetched, None, None
        return fetched

    def tie(self, before, received, room, fetch=False):
        while True:
            self.pieces = [p for p in self.pieces if not p.done]
            fitting = [p for p in self.pieces if p.cost <= 2 * room]
            if not fitting:
                return received
            piece = fitting[0]
            room -= piece.cost
            if fetch and self.wanted and piece.fetches:
                made = piece.run(before, self.wanted)
                self.wanted, self.fetched = None, made[-1]
                made = made[:-1]
            else:
                made = piece.run(before)
                made = made[:-1] if piece.fetches else made
            received, _ = lax.optimization_barrier((received, made))

    def rest(self):
        for piece in self.pieces:
            piece.run(None)


def after(value, before):
    if before is None:
        return value
    return lax.optimization_barrier((value, before))[0]


def swap(value, axis, mask):
    size = lax.axis_size(axis)
    return lax.ppermute(value, axis, [(i, i ^ mask) for i in range(size)])


def added(left, right):
    return left.astype(f32) + right.astype(f32)


def col_steps():
    bits = lax.axis_size("col").bit_length() - 1
    place = lax.axis_index("col")
    bit = [(place >> j) & 1 for j in range(bits)]
    masks = [1 << j for j in range(bits)]
    if bits >= 3:
        bit[bits - 2] = bit[bits - 2] ^ bit[bits - 1]
        masks[-1] += masks[-2]
    return masks, bit


def packed(bits):
    number = jnp.int32(0)
    for b in bits:
        number = number * 2 + b
    return number


def row_sum(partial, work):
    bits = lax.axis_size("row").bit_length() - 1
    parts = [partial[p] for p in range(partial.shape[0])]
    orders = [list(range(bits)), list(range(bits))[::-1]]
    for j in range(bits):
        received = [swap(p, "row", 1 << o[j]) for p, o in zip(parts, orders)]
        received = work.tie(parts, received, row_room, j == bits - 1)
        parts = [added(p, r) for p, r in zip(parts, received)]
        if j < bits - 1:
            parts = [p.astype(bf16) for p in parts]
    return jnp.concatenate(parts, axis=0)


def subtracted(own, total, work):
    masks, _ = col_steps()
    for j, mask in enumerate(masks[:-1]):
        half = total.shape[0] // 2
        mine, other = total[:half], total[half:]
        received = work.tie(other, swap(other, "col", mask), core_room if j == 0 else near_room)
        total = added(mine, received).astype(bf16)
    received = work.tie(total, swap(total, "col", masks[-1]), far_room)
    value = (own.astype(f32) - added(total, received)).astype(bf16)
    for j, mask in reversed(list(enumerate(masks[:-1]))):
        received = work.tie(
            value, swap(value, "col", mask), core_room if j == 0 else near_room, True
        )
        value = jnp.concatenate([value, received], axis=0)
    return value


def scattered(total):
    masks, _ = col_steps()
    for j, mask in enumerate(masks):
        half = total.shape[0] // 2
        total = added(total[:half], swap(total[half:], "col", mask))
        if j < len(masks) - 1:
            total = total.astype(bf16)
    return total[0]


def shards(factor_blocks, inverse_blocks, right_side, centers, owner_map, test_pool, test_rows):
    panels = inverse_blocks.shape[0]
    col_tiles = inverse_blocks.shape[1]
    tile_size = inverse_blocks.shape[2]
    row_tiles = inverse_blocks.shape[3]
    width_out = right_side.shape[3]
    own_rows = row_tiles * tile_size
    tests = test_rows.shape[0]
    chunks = 4
    chunk = tests // chunks
    group = chunks

    _, kept = col_steps()
    parts = 2 ** (len(kept) - 1)
    flip = packed(kept[:-1])
    flip_ref = flip.reshape(1)
    targets = right_side.reshape(panels, parts, own_rows // parts, width_out)
    size = 2 ** len(kept)
    blocks = np.arange(size)
    digits = [(blocks >> j) & 1 for j in range(len(kept))]
    if len(kept) >= 3:
        digits[-2] = digits[-2] ^ digits[-1]
    places = sum(d << (len(kept) - 1 - j) for j, d in enumerate(digits)).astype(np.int32)
    places = jnp.asarray(places) ^ packed(kept)

    work = Beside()
    span = [None] * chunks
    norms = [None] * chunks
    center_sq = [None] * panels
    first = [None] * chunks
    totals = [None] * chunks
    solved = [None] * panels
    rounded = [None] * panels
    partial = [None] * panels

    tiles = owner_map.shape[0]
    match = owner_map == jnp.arange(tiles, dtype=jnp.int32)[None, :]
    slots = jnp.sum(match * jnp.arange(tiles, dtype=jnp.int32)[:, None], axis=0)
    located = test_rows - lax.axis_index("row") * test_pool.shape[0]

    def gather(i, count):
        def make(before):
            made = gathered(
                after(located[i * chunk : (i + count) * chunk], before), test_pool, count, f"gathered_{i}"
            )
            span[i : i + count] = made[:count]
            norms[i : i + count] = made[count:]
            return made

        return Piece(min(1.3 + 2.6 * count, 6.0), make)

    def panel_slots(k, before):
        return after(slots[k * col_tiles : (k + 1) * col_tiles], before)

    def score(k, i):
        def make(before, fetch=None):
            made, center_sq[k], fetched = scored(
                span[i], norms[i], centers, center_sq[k], panel_slots(k, before),
                rounded[k] if k > 0 else None, totals[i] if k > 0 else None, fetch,
                f"scored_{k}_{i}",
            )
            if k > 0:
                totals[i] = made
            else:
                first[i] = made
            return made, fetched

        return Piece(2.9 if k > 0 else 2.7, make, True)

    def factor(early, k, kept=None):
        def make(before):
            partial[early] = panel_product(
                factor_blocks,
                pair_slot(early, k),
                kept,
                after(rounded[k], before)[None],
                None,
                partial[early],
                parts,
                flip_ref,
                bf16 if early == k - 1 else f32,
                f"factor_{early}_{k}",
            )
            return partial[early]

        return Piece(3.6, make)

    work.pieces += [gather(i, group) for i in range(0, chunks, group)]
    ahead = []
    for k in range(panels - 1, -1, -1):
        if k == panels - 1:
            residue, residue_flip = targets[k], None
        else:
            for early, piece in ahead:
                if early == k:
                    piece.run(None)
            factor(k, k + 1, work.take()).run(None)
            own = lax.dynamic_slice(
                targets, (k, flip, 0, 0), (1, 1) + targets.shape[2:]
            )[0]
            residue, residue_flip = subtracted(own, partial[k], work), flip_ref
        product = panel_product(
            inverse_blocks, k, work.take(), residue, residue_flip, None, row_parts, None, bf16,
            f"inverse_{k}",
        )
        if k > 0:
            work.want((factor_blocks, pair_slot(k - 1, k)))
        solved[k] = row_sum(product, work)
        rounded[k] = solved[k].astype(bf16)
        early = [(e, factor(e, k)) for e in range(k - 2, -1, -1)]
        ahead += early
        if k == panels - 1:
            work.pieces += [score(0, i) for i in range(chunks)]
        if k > 0:
            place = len(work.pieces) - (0 if k == 1 else chunks)
            place = max(place, 0)
            later = [score(k, i) for i in range(chunks)]
            early = [piece for _, piece in early]
            work.pieces[place:place] = early[:1] + later + early[1:]
    work.rest()
    estimate = scattered(finished(first, rounded[0], totals, places))
    alpha = jnp.stack(solved).reshape(panels, col_tiles, tile_size, width_out)
    return (alpha, estimate)


def solution(mesh):
    in_specs = (
        P(None, None, "row", None, "col"),
        P(None, None, "col", None, "row"),
        P(None, None, "row", None),
        P(None, "col", None),
        P(None, "col"),
        P("row", None),
        P("row"),
    )
    out_specs = (P(None, None, "col", None), P(("row", "col"), None))
    return jax.shard_map(shards, mesh=mesh, in_specs=in_specs, out_specs=out_specs, check_vma=False)
```

```python
import math

import jax
import jax.numpy as jnp
import numpy as np
from jax import lax
from jax.experimental import pallas as pl
from jax.experimental.pallas import tpu as pltpu
from jax.sharding import PartitionSpec as P

inverse_width = 0.35
log2e = math.log2(math.e)
scale = -inverse_width * log2e
row_room, core_room, near_room, far_room = 3.3, 1.2, 3.0, 5.5
row_parts = 2
flying = 8
bf16 = jnp.bfloat16
f32 = jnp.float32
vmem = pl.BlockSpec(memory_space=pltpu.VMEM)
smem = pl.BlockSpec(memory_space=pltpu.SMEM)
stays = pl.BlockSpec(memory_space=pltpu.HBM)


def params(mib):
    return pltpu.CompilerParams(vmem_limit_bytes=mib * 2**20)


def pair_slot(early, successor):
    return successor * (successor - 1) // 2 + early


def fetches(block_ref, slot, held, sem):
    return [
        pltpu.make_async_copy(block_ref.at[slot, g], held.at[g], sem.at[g])
        for g in range(held.shape[0])
    ]


def panel_product(blocks, slot, kept, vector, vector_flip, earlier, out_parts, out_flip, out_dtype, name):
    _, groups, rows, inner, width = blocks.shape
    depth = inner * width
    out_width = vector.shape[-1]
    in_parts = vector.shape[0]
    part_rows = groups * rows // out_parts
    unit = min(rows, part_rows)
    flips = [f for f in (vector_flip, out_flip) if f is not None]
    more = [] if earlier is None else [earlier]

    def body(*refs):
        flip_refs, refs = list(refs[: len(flips)]), refs[len(flips) :]
        block_ref, vector_ref = refs[:2]
        out_ref = refs[2 + len(more)]
        held, sem = refs[3 + len(more) :] if kept is None else (block_ref, None)
        in_flip = 0 if vector_flip is None else flip_refs.pop(0)[0]
        flip = 0 if out_flip is None else flip_refs.pop(0)[0]
        copies = []
        if kept is None:
            copies = fetches(block_ref, slot, held, sem)
        for copy in copies[:flying]:
            copy.start()
        if in_parts == 1:
            column = vector_ref[0]
        elif vector_flip is None:
            column = vector_ref[...].reshape(depth, out_width)
        else:
            column = jnp.concatenate([vector_ref[p ^ in_flip] for p in range(in_parts)], axis=0)
        for g in range(groups):
            if kept is None:
                copies[g].wait()
                for copy in copies[g + flying : g + flying + 1]:
                    copy.start()
            for u in range(rows // unit):
                part, at = divmod(g * rows + u * unit, part_rows)
                at = pl.ds(at, unit)
                value = jnp.dot(
                    held[g, u * unit : (u + 1) * unit].reshape(unit, depth),
                    column,
                    preferred_element_type=f32,
                )
                if more:
                    value = value + refs[2][part ^ flip, at, :]
                out_ref[part ^ flip, at, :] = value.astype(out_dtype)

    source = pltpu.with_memory_space_constraint(blocks, pltpu.HBM) if kept is None else kept
    return pl.pallas_call(
        body,
        in_specs=[smem] * len(flips) + [stays if kept is None else vmem] + [vmem] * (1 + len(more)),
        out_specs=vmem,
        out_shape=jax.ShapeDtypeStruct((out_parts, part_rows, out_width), out_dtype),
        scratch_shapes=[
            pltpu.VMEM((groups, rows, inner, width), bf16),
            pltpu.SemaphoreType.DMA((groups,)),
        ]
        if kept is None
        else [],
        compiler_params=params(8),
        cost_estimate=pl.CostEstimate(
            flops=4 * groups * rows * depth * out_width,
            bytes_accessed=2 * groups * rows * depth,
            transcendentals=0,
        ),
        name=name,
    )(*flips, source, vector, *more)


def gathered(located, pool, chunks, name):
    count = located.shape[0]
    rows, dim = pool.shape
    cuts = dim // 128
    chunk = count // chunks
    group = 64
    step = 128
    block = min(1024, rows)
    stages = min(6, rows // block)

    def body(located_ref, pool_ref, *refs):
        out_refs, norm_refs = refs[:chunks], refs[chunks : 2 * chunks]
        wide, held, staged, sem, rows_out, norms_out, out_sem = refs[2 * chunks :]
        copies = [
            pltpu.make_async_copy(
                pool_ref.at[pl.ds(b * block, block)], staged.at[b % stages], sem.at[b % stages]
            )
            for b in range(rows // block)
        ]

        def widen(b):
            def convert(i, carry):
                at = pl.multiple_of(i * step, step)
                value = staged[b % stages, pl.ds(at, step), :].astype(f32)
                for h in range(cuts):
                    to = pl.ds((b * block + at) * cuts + h, step, stride=cuts)
                    wide[to, :] = value[:, h * 128 : (h + 1) * 128]
                return carry

            lax.fori_loop(0, block // step, convert, 0)

        def part(j):
            def fetch(i, carry):
                for u in range(group):
                    at = i * group + u
                    source = pl.multiple_of(located_ref[j * chunk + at], cuts)
                    held[pl.ds(pl.multiple_of(at * cuts, cuts), cuts), :] = wide[pl.ds(source, cuts), :]
                return carry

            def store(i, carry):
                at = pl.multiple_of(i * step, step)
                parts = [held[pl.ds(at * cuts + h, step, stride=cuts), :] for h in range(cuts)]
                rows_out[j % 2, pl.ds(at, step), :] = jnp.concatenate(parts, axis=1).astype(bf16)
                total = sum(p * p for p in parts)
                norm = scale * jnp.sum(total, axis=1, keepdims=True)
                norms_out[j % 2, pl.ds(at, step), :] = jnp.broadcast_to(norm, (step, 128))
                return carry

            lax.fori_loop(0, chunk // group, fetch, 0)
            lax.fori_loop(0, chunk // step, store, 0)

        for copy in copies[:stages]:
            copy.start()
        for b in range(len(copies)):
            copies[b].wait()
            widen(b)
            for copy in copies[b + stages : b + stages + 1]:
                copy.start()
        writes = []
        for j in range(chunks):
            for copy in writes[2 * (j - 2) : 2 * (j - 1)] if j >= 2 else []:
                copy.wait()
            part(j)
            for n, (source, to) in enumerate(((rows_out, out_refs), (norms_out, norm_refs))):
                writes.append(pltpu.make_async_copy(source.at[j % 2], to[j], out_sem.at[j % 2, n]))
                writes[-1].start()
        for copy in writes[2 * max(chunks - 2, 0) :]:
            copy.wait()

    return pl.pallas_call(
        body,
        in_specs=[smem, stays],
        out_specs=[stays] * (2 * chunks),
        out_shape=[pltpu.HBM((chunk, dim), bf16)] * chunks + [pltpu.HBM((chunk, 128), f32)] * chunks,
        scratch_shapes=[
            pltpu.VMEM((rows * cuts, 128), f32),
            pltpu.VMEM((chunk * cuts, 128), f32),
            pltpu.VMEM((stages, block, dim), bf16),
            pltpu.SemaphoreType.DMA((stages,)),
            pltpu.VMEM((2, chunk, dim), bf16),
            pltpu.VMEM((2, chunk, 128), f32),
            pltpu.SemaphoreType.DMA((2, 2)),
        ],
        compiler_params=params(28),
        cost_estimate=pl.CostEstimate(
            flops=0, bytes_accessed=6 * rows * dim + 16 * count * dim, transcendentals=0
        ),
        name=name,
    )(located * cuts, pltpu.with_memory_space_constraint(pool, pltpu.HBM))


def scored(span, norms, centers, center_sq, slots, weights, earlier, fetch, name):
    tests, dim = span.shape
    tiles = slots.shape[0]
    size = centers.shape[1]
    step = min(512 if weights is not None else 256, tests)
    steps = tests // step
    depth = tiles * size
    more = [x for x in (weights, earlier) if x is not None]
    fresh = center_sq is None

    def body(slots_ref, span_ref, norm_ref, center_ref, *refs):
        refs = list(refs)
        sq_ref = None if fresh else refs.pop(0)
        more_refs = [refs.pop(0) for _ in more]
        source = None if fetch is None else refs.pop(0)
        out_ref = refs.pop(0)
        if fresh:
            sq_ref = refs.pop(0)
        copies = []
        if fetch is not None:
            copies = fetches(source, fetch[1], refs.pop(0), refs.pop())
            for copy in copies:
                copy.start()
        if fresh:
            for t in range(tiles):
                value = center_ref[slots_ref[t]].astype(f32)
                sq_ref[t] = scale * jnp.sum(value * value, axis=1, keepdims=True).T
        writes = []
        if weights is None:
            values, sem = refs
            writes = [
                pltpu.make_async_copy(values.at[i], out_ref.at[pl.ds(i * step, step)], sem.at[i])
                for i in range(steps)
            ]
        for i in range(steps):
            at = slice(i * step, (i + 1) * step)
            rows = span_ref[at, :]
            norm = jnp.concatenate([norm_ref[at, :]] * (size // 128), axis=1)
            row_values = []
            for t in range(tiles):
                slot = slots_ref[t]
                crossed = lax.dot_general(
                    rows, center_ref[slot], (((1,), (1,)), ((), ())), preferred_element_type=f32
                )
                value = jnp.exp2((crossed * (-2.0 * scale) + sq_ref[t]) + norm).astype(bf16)
                if weights is None:
                    values[i, :, t * size : (t + 1) * size] = value
                else:
                    row_values.append(value)
            if weights is None:
                writes[i].start()
            else:
                total = jnp.dot(
                    jnp.concatenate(row_values, axis=1), more_refs[0][...], preferred_element_type=f32
                )
                out_ref[at, :] = total if earlier is None else total + more_refs[1][at, :]
        for copy in writes + copies:
            copy.wait()

    if weights is None:
        out_shapes, out_specs = [jax.ShapeDtypeStruct((tests, depth), bf16)], [stays]
        scratch = [pltpu.VMEM((steps, step, depth), bf16), pltpu.SemaphoreType.DMA((steps,))]
    else:
        out_shapes, out_specs = [jax.ShapeDtypeStruct((tests, weights.shape[1]), f32)], [vmem]
        scratch = []
    operands = [slots, span, norms, centers] + ([] if fresh else [center_sq]) + more
    in_specs = [smem] + [vmem] * (len(operands) - 1)
    if fresh:
        out_shapes = out_shapes + [jax.ShapeDtypeStruct((tiles, 1, size), f32)]
        out_specs = out_specs + [vmem]
    if fetch is not None:
        in_specs = in_specs + [stays]
        operands = operands + [pltpu.with_memory_space_constraint(fetch[0], pltpu.HBM)]
        out_shapes = out_shapes + [jax.ShapeDtypeStruct(fetch[0].shape[1:], fetch[0].dtype)]
        out_specs = out_specs + [vmem]
        scratch = scratch + [pltpu.SemaphoreType.DMA((fetch[0].shape[1],))]
    if weights is None:
        out_shapes[0] = pltpu.HBM(out_shapes[0].shape, out_shapes[0].dtype)
    made = pl.pallas_call(
        body,
        in_specs=in_specs,
        out_specs=out_specs,
        out_shape=out_shapes,
        scratch_shapes=scratch,
        compiler_params=params(8),
        cost_estimate=pl.CostEstimate(
            flops=3 * tests * depth * dim,
            bytes_accessed=2 * tests * dim,
            transcendentals=tests * depth,
        ),
        name=name,
    )(*operands)
    sq = made[1] if fresh else center_sq
    return made[0], sq, made[-1] if fetch is not None else None


def finished(kernels, weights, totals, places):
    blocks = places.shape[0]
    tests, depth = kernels[0].shape
    width = weights.shape[1]
    height = len(kernels) * tests // blocks
    unit = min(height, tests)

    def body(places_ref, *refs):
        kernel_refs, weight_ref = refs[: len(kernels)], refs[len(kernels)]
        total_refs, out_ref = refs[len(kernels) + 1 : -1], refs[-1]
        for start in range(0, blocks * height, unit):
            c, at = divmod(start, tests)
            block, within = divmod(start, height)
            value = jnp.dot(
                kernel_refs[c][at : at + unit, :], weight_ref[...], preferred_element_type=f32
            )
            value = value + total_refs[c][at : at + unit, :]
            out_ref[places_ref[block], within : within + unit, :] = value.astype(bf16)

    return pl.pallas_call(
        body,
        in_specs=[smem] + [vmem] * (len(kernels) + 1 + len(totals)),
        out_specs=vmem,
        out_shape=jax.ShapeDtypeStruct((blocks, height, width), bf16),
        compiler_params=params(8),
        cost_estimate=pl.CostEstimate(
            flops=4 * blocks * height * depth * width,
            bytes_accessed=2 * blocks * height * depth,
            transcendentals=0,
        ),
        name="finished",
    )(places, *kernels, weights, *totals)


class Piece:
    def __init__(self, cost, make, fetches=False):
        self.cost, self.make, self.done, self.fetches = cost, make, False, fetches

    def run(self, before, fetch=None):
        if not self.done:
            self.done = True
            return self.make(before, fetch) if fetch else self.make(before)


class Beside:
    def __init__(self):
        self.pieces = []
        self.wanted = None
        self.fetched = None

    def want(self, wanted):
        self.wanted, self.fetched = wanted, None

    def take(self):
        fetched, self.wanted, self.fetched = self.fetched, None, None
        return fetched

    def tie(self, before, received, room, fetch=False):
        while True:
            self.pieces = [p for p in self.pieces if not p.done]
            fitting = [p for p in self.pieces if p.cost <= 2 * room]
            if not fitting:
                return received
            piece = fitting[0]
            room -= piece.cost
            if fetch and self.wanted and piece.fetches:
                made = piece.run(before, self.wanted)
                self.wanted, self.fetched = None, made[-1]
                made = made[:-1]
            else:
                made = piece.run(before)
                made = made[:-1] if piece.fetches else made
            received, _ = lax.optimization_barrier((received, made))

    def rest(self):
        for piece in self.pieces:
            piece.run(None)


def after(value, before):
    if before is None:
        return value
    return lax.optimization_barrier((value, before))[0]


def swap(value, axis, mask):
    size = lax.axis_size(axis)
    return lax.ppermute(value, axis, [(i, i ^ mask) for i in range(size)])


def added(left, right):
    return left.astype(f32) + right.astype(f32)


def col_steps():
    bits = lax.axis_size("col").bit_length() - 1
    place = lax.axis_index("col")
    bit = [(place >> j) & 1 for j in range(bits)]
    masks = [1 << j for j in range(bits)]
    if bits >= 3:
        bit[bits - 2] = bit[bits - 2] ^ bit[bits - 1]
        masks[-1] += masks[-2]
    return masks, bit


def packed(bits):
    number = jnp.int32(0)
    for b in bits:
        number = number * 2 + b
    return number


def row_sum(partial, work):
    bits = lax.axis_size("row").bit_length() - 1
    parts = [partial[p] for p in range(partial.shape[0])]
    orders = [list(range(bits)), list(range(bits))[::-1]]
    for j in range(bits):
        received = [swap(p, "row", 1 << o[j]) for p, o in zip(parts, orders)]
        received = work.tie(parts, received, row_room, j == bits - 1)
        parts = [added(p, r) for p, r in zip(parts, received)]
        if j < bits - 1:
            parts = [p.astype(bf16) for p in parts]
    return jnp.concatenate(parts, axis=0)


def subtracted(own, total, work):
    masks, _ = col_steps()
    for j, mask in enumerate(masks[:-1]):
        half = total.shape[0] // 2
        mine, other = total[:half], total[half:]
        received = work.tie(other, swap(other, "col", mask), core_room if j == 0 else near_room)
        total = added(mine, received).astype(bf16)
    received = work.tie(total, swap(total, "col", masks[-1]), far_room)
    value = (own.astype(f32) - added(total, received)).astype(bf16)
    for j, mask in reversed(list(enumerate(masks[:-1]))):
        received = work.tie(
            value, swap(value, "col", mask), core_room if j == 0 else near_room, True
        )
        value = jnp.concatenate([value, received], axis=0)
    return value


def scattered(total):
    masks, _ = col_steps()
    for j, mask in enumerate(masks):
        half = total.shape[0] // 2
        total = added(total[:half], swap(total[half:], "col", mask))
        if j < len(masks) - 1:
            total = total.astype(bf16)
    return total[0]


def shards(factor_blocks, inverse_blocks, right_side, centers, owner_map, test_pool, test_rows):
    panels = inverse_blocks.shape[0]
    col_tiles = inverse_blocks.shape[1]
    tile_size = inverse_blocks.shape[2]
    row_tiles = inverse_blocks.shape[3]
    width_out = right_side.shape[3]
    own_rows = row_tiles * tile_size
    tests = test_rows.shape[0]
    chunks = 4
    chunk = tests // chunks
    group = chunks

    _, kept = col_steps()
    parts = 2 ** (len(kept) - 1)
    flip = packed(kept[:-1])
    flip_ref = flip.reshape(1)
    targets = right_side.reshape(panels, parts, own_rows // parts, width_out)
    size = 2 ** len(kept)
    blocks = np.arange(size)
    digits = [(blocks >> j) & 1 for j in range(len(kept))]
    if len(kept) >= 3:
        digits[-2] = digits[-2] ^ digits[-1]
    places = sum(d << (len(kept) - 1 - j) for j, d in enumerate(digits)).astype(np.int32)
    places = jnp.asarray(places) ^ packed(kept)

    work = Beside()
    span = [None] * chunks
    norms = [None] * chunks
    center_sq = [None] * panels
    first = [None] * chunks
    totals = [None] * chunks
    solved = [None] * panels
    rounded = [None] * panels
    partial = [None] * panels

    tiles = owner_map.shape[0]
    match = owner_map == jnp.arange(tiles, dtype=jnp.int32)[None, :]
    slots = jnp.sum(match * jnp.arange(tiles, dtype=jnp.int32)[:, None], axis=0)
    located = test_rows - lax.axis_index("row") * test_pool.shape[0]

    def gather(i, count):
        def make(before):
            made = gathered(
                after(located[i * chunk : (i + count) * chunk], before), test_pool, count, f"gathered_{i}"
            )
            span[i : i + count] = made[:count]
            norms[i : i + count] = made[count:]
            return made

        return Piece(min(1.3 + 2.6 * count, 6.0), make)

    def panel_slots(k, before):
        return after(slots[k * col_tiles : (k + 1) * col_tiles], before)

    def score(k, i):
        def make(before, fetch=None):
            made, center_sq[k], fetched = scored(
                span[i], norms[i], centers, center_sq[k], panel_slots(k, before),
                rounded[k] if k > 0 else None, totals[i] if k > 0 else None, fetch,
                f"scored_{k}_{i}",
            )
            if k > 0:
                totals[i] = made
            else:
                first[i] = made
            return made, fetched

        return Piece(2.5 if k > 0 else 2.7, make, True)

    def factor(early, k, kept=None):
        def make(before):
            partial[early] = panel_product(
                factor_blocks,
                pair_slot(early, k),
                kept,
                after(rounded[k], before)[None],
                None,
                partial[early],
                parts,
                flip_ref,
                bf16 if early == k - 1 else f32,
                f"factor_{early}_{k}",
            )
            return partial[early]

        return Piece(3.6, make)

    work.pieces += [gather(i, group) for i in range(0, chunks, group)]
    work.pieces += [score(0, i) for i in range(chunks)]
    ahead = []
    for k in range(panels - 1, -1, -1):
        if k == panels - 1:
            residue, residue_flip = targets[k], None
        else:
            for early, piece in ahead:
                if early == k:
                    piece.run(None)
            factor(k, k + 1, work.take()).run(None)
            if k > 0:
                work.want((inverse_blocks, k))
            own = lax.dynamic_slice(
                targets, (k, flip, 0, 0), (1, 1) + targets.shape[2:]
            )[0]
            residue, residue_flip = subtracted(own, partial[k], work), flip_ref
        product = panel_product(
            inverse_blocks, k, work.take(), residue, residue_flip, None, row_parts, None, bf16,
            f"inverse_{k}",
        )
        if k > 0:
            work.want((factor_blocks, pair_slot(k - 1, k)))
        solved[k] = row_sum(product, work)
        rounded[k] = solved[k].astype(bf16)
        early = [(e, factor(e, k)) for e in range(k - 2, -1, -1)]
        ahead += early
        if k > 0:
            early = [piece for _, piece in early]
            work.pieces[:0] = early[:1]
            work.pieces += early[1:] + [score(k, i) for i in range(chunks)]
    work.rest()
    estimate = scattered(finished(first, rounded[0], totals, places))
    alpha = jnp.stack(solved).reshape(panels, col_tiles, tile_size, width_out)
    return (alpha, estimate)


def solution(mesh):
    in_specs = (
        P(None, None, "row", None, "col"),
        P(None, None, "col", None, "row"),
        P(None, None, "row", None),
        P(None, "col", None),
        P(None, "col"),
        P("row", None),
        P("row"),
    )
    out_specs = (P(None, None, "col", None), P(("row", "col"), None))
    return jax.shard_map(shards, mesh=mesh, in_specs=in_specs, out_specs=out_specs, check_vma=False)
```

```python
import math

import jax
import jax.numpy as jnp
import numpy as np
from jax import lax
from jax.experimental import pallas as pl
from jax.experimental.pallas import tpu as pltpu
from jax.sharding import PartitionSpec as P

inverse_width = 0.35
log2e = math.log2(math.e)
scale = -inverse_width * log2e
row_room, core_room, near_room, far_room = 3.3, 1.2, 3.0, 5.5
row_parts = 2
flying = 8
bf16 = jnp.bfloat16
f32 = jnp.float32
vmem = pl.BlockSpec(memory_space=pltpu.VMEM)
smem = pl.BlockSpec(memory_space=pltpu.SMEM)
stays = pl.BlockSpec(memory_space=pltpu.HBM)


def params(mib):
    return pltpu.CompilerParams(vmem_limit_bytes=mib * 2**20)


def pair_slot(early, successor):
    return successor * (successor - 1) // 2 + early


def fetches(block_ref, slot, held, sem):
    return [
        pltpu.make_async_copy(block_ref.at[slot, g], held.at[g], sem.at[g])
        for g in range(held.shape[0])
    ]


def panel_product(blocks, slot, kept, vector, vector_flip, earlier, out_parts, out_flip, out_dtype, name):
    _, groups, rows, inner, width = blocks.shape
    depth = inner * width
    out_width = vector.shape[-1]
    in_parts = vector.shape[0]
    part_rows = groups * rows // out_parts
    unit = min(rows, part_rows)
    flips = [f for f in (vector_flip, out_flip) if f is not None]
    more = [] if earlier is None else [earlier]

    def body(*refs):
        flip_refs, refs = list(refs[: len(flips)]), refs[len(flips) :]
        block_ref, vector_ref = refs[:2]
        out_ref = refs[2 + len(more)]
        held, sem = refs[3 + len(more) :] if kept is None else (block_ref, None)
        in_flip = 0 if vector_flip is None else flip_refs.pop(0)[0]
        flip = 0 if out_flip is None else flip_refs.pop(0)[0]
        copies = []
        if kept is None:
            copies = fetches(block_ref, slot, held, sem)
        for copy in copies[:flying]:
            copy.start()
        if in_parts == 1:
            column = vector_ref[0]
        elif vector_flip is None:
            column = vector_ref[...].reshape(depth, out_width)
        else:
            column = jnp.concatenate([vector_ref[p ^ in_flip] for p in range(in_parts)], axis=0)
        for g in range(groups):
            if kept is None:
                copies[g].wait()
                for copy in copies[g + flying : g + flying + 1]:
                    copy.start()
            for u in range(rows // unit):
                part, at = divmod(g * rows + u * unit, part_rows)
                at = pl.ds(at, unit)
                value = jnp.dot(
                    held[g, u * unit : (u + 1) * unit].reshape(unit, depth),
                    column,
                    preferred_element_type=f32,
                )
                if more:
                    value = value + refs[2][part ^ flip, at, :]
                out_ref[part ^ flip, at, :] = value.astype(out_dtype)

    source = pltpu.with_memory_space_constraint(blocks, pltpu.HBM) if kept is None else kept
    return pl.pallas_call(
        body,
        in_specs=[smem] * len(flips) + [stays if kept is None else vmem] + [vmem] * (1 + len(more)),
        out_specs=vmem,
        out_shape=jax.ShapeDtypeStruct((out_parts, part_rows, out_width), out_dtype),
        scratch_shapes=[
            pltpu.VMEM((groups, rows, inner, width), bf16),
            pltpu.SemaphoreType.DMA((groups,)),
        ]
        if kept is None
        else [],
        compiler_params=params(8),
        cost_estimate=pl.CostEstimate(
            flops=4 * groups * rows * depth * out_width,
            bytes_accessed=2 * groups * rows * depth,
            transcendentals=0,
        ),
        name=name,
    )(*flips, source, vector, *more)


def gathered(located, pool, chunks, name):
    count = located.shape[0]
    rows, dim = pool.shape
    cuts = dim // 128
    chunk = count // chunks
    group = 64
    step = 128
    block = min(1024, rows)
    stages = min(6, rows // block)

    def body(located_ref, pool_ref, *refs):
        out_refs, norm_refs = refs[:chunks], refs[chunks : 2 * chunks]
        wide, held, staged, sem, rows_out, norms_out, out_sem = refs[2 * chunks :]
        copies = [
            pltpu.make_async_copy(
                pool_ref.at[pl.ds(b * block, block)], staged.at[b % stages], sem.at[b % stages]
            )
            for b in range(rows // block)
        ]

        def widen(b):
            def convert(i, carry):
                at = pl.multiple_of(i * step, step)
                value = staged[b % stages, pl.ds(at, step), :].astype(f32)
                for h in range(cuts):
                    to = pl.ds((b * block + at) * cuts + h, step, stride=cuts)
                    wide[to, :] = value[:, h * 128 : (h + 1) * 128]
                return carry

            lax.fori_loop(0, block // step, convert, 0)

        def part(j):
            def fetch(i, carry):
                for u in range(group):
                    at = i * group + u
                    source = pl.multiple_of(located_ref[j * chunk + at], cuts)
                    held[pl.ds(pl.multiple_of(at * cuts, cuts), cuts), :] = wide[pl.ds(source, cuts), :]
                return carry

            def store(i, carry):
                at = pl.multiple_of(i * step, step)
                parts = [held[pl.ds(at * cuts + h, step, stride=cuts), :] for h in range(cuts)]
                rows_out[j % 2, pl.ds(at, step), :] = jnp.concatenate(parts, axis=1).astype(bf16)
                total = sum(p * p for p in parts)
                norm = scale * jnp.sum(total, axis=1, keepdims=True)
                norms_out[j % 2, pl.ds(at, step), :] = jnp.broadcast_to(norm, (step, 128))
                return carry

            lax.fori_loop(0, chunk // group, fetch, 0)
            lax.fori_loop(0, chunk // step, store, 0)

        for copy in copies[:stages]:
            copy.start()
        for b in range(len(copies)):
            copies[b].wait()
            widen(b)
            for copy in copies[b + stages : b + stages + 1]:
                copy.start()
        writes = []
        for j in range(chunks):
            for copy in writes[2 * (j - 2) : 2 * (j - 1)] if j >= 2 else []:
                copy.wait()
            part(j)
            for n, (source, to) in enumerate(((rows_out, out_refs), (norms_out, norm_refs))):
                writes.append(pltpu.make_async_copy(source.at[j % 2], to[j], out_sem.at[j % 2, n]))
                writes[-1].start()
        for copy in writes[2 * max(chunks - 2, 0) :]:
            copy.wait()

    return pl.pallas_call(
        body,
        in_specs=[smem, stays],
        out_specs=([vmem] + [stays] * (chunks - 1)) * 2,
        out_shape=[
            (jax.ShapeDtypeStruct if j == 0 else pltpu.HBM)((chunk, width), kind)
            for width, kind in ((dim, bf16), (128, f32))
            for j in range(chunks)
        ],
        scratch_shapes=[
            pltpu.VMEM((rows * cuts, 128), f32),
            pltpu.VMEM((chunk * cuts, 128), f32),
            pltpu.VMEM((stages, block, dim), bf16),
            pltpu.SemaphoreType.DMA((stages,)),
            pltpu.VMEM((2, chunk, dim), bf16),
            pltpu.VMEM((2, chunk, 128), f32),
            pltpu.SemaphoreType.DMA((2, 2)),
        ],
        compiler_params=params(28),
        cost_estimate=pl.CostEstimate(
            flops=0, bytes_accessed=6 * rows * dim + 16 * count * dim, transcendentals=0
        ),
        name=name,
    )(located * cuts, pltpu.with_memory_space_constraint(pool, pltpu.HBM))


def scored(span, norms, centers, center_sq, slots, weights, earlier, fetch, name):
    tests, dim = span.shape
    tiles = slots.shape[0]
    size = centers.shape[1]
    step = min(512 if weights is not None else 256, tests)
    steps = tests // step
    depth = tiles * size
    more = [x for x in (weights, earlier) if x is not None]
    fresh = center_sq is None

    def body(slots_ref, span_ref, norm_ref, center_ref, *refs):
        refs = list(refs)
        sq_ref = None if fresh else refs.pop(0)
        more_refs = [refs.pop(0) for _ in more]
        source = None if fetch is None else refs.pop(0)
        out_ref = refs.pop(0)
        if fresh:
            sq_ref = refs.pop(0)
        copies = []
        if fetch is not None:
            copies = fetches(source, fetch[1], refs.pop(0), refs.pop())
            for copy in copies:
                copy.start()
        if fresh:
            for t in range(tiles):
                value = center_ref[slots_ref[t]].astype(f32)
                sq_ref[t] = scale * jnp.sum(value * value, axis=1, keepdims=True).T
        writes = []
        if weights is None:
            values, sem = refs
            writes = [
                pltpu.make_async_copy(values.at[i], out_ref.at[pl.ds(i * step, step)], sem.at[i])
                for i in range(steps)
            ]
        for i in range(steps):
            at = slice(i * step, (i + 1) * step)
            rows = span_ref[at, :]
            norm = jnp.concatenate([norm_ref[at, :]] * (size // 128), axis=1)
            row_values = []
            for t in range(tiles):
                slot = slots_ref[t]
                crossed = lax.dot_general(
                    rows, center_ref[slot], (((1,), (1,)), ((), ())), preferred_element_type=f32
                )
                value = jnp.exp2((crossed * (-2.0 * scale) + sq_ref[t]) + norm).astype(bf16)
                if weights is None:
                    values[i, :, t * size : (t + 1) * size] = value
                else:
                    row_values.append(value)
            if weights is None:
                writes[i].start()
            else:
                total = jnp.dot(
                    jnp.concatenate(row_values, axis=1), more_refs[0][...], preferred_element_type=f32
                )
                out_ref[at, :] = total if earlier is None else total + more_refs[1][at, :]
        for copy in writes + copies:
            copy.wait()

    if weights is None:
        out_shapes, out_specs = [jax.ShapeDtypeStruct((tests, depth), bf16)], [stays]
        scratch = [pltpu.VMEM((steps, step, depth), bf16), pltpu.SemaphoreType.DMA((steps,))]
    else:
        out_shapes, out_specs = [jax.ShapeDtypeStruct((tests, weights.shape[1]), f32)], [vmem]
        scratch = []
    operands = [slots, span, norms, centers] + ([] if fresh else [center_sq]) + more
    in_specs = [smem] + [vmem] * (len(operands) - 1)
    if fresh:
        out_shapes = out_shapes + [jax.ShapeDtypeStruct((tiles, 1, size), f32)]
        out_specs = out_specs + [vmem]
    if fetch is not None:
        in_specs = in_specs + [stays]
        operands = operands + [pltpu.with_memory_space_constraint(fetch[0], pltpu.HBM)]
        out_shapes = out_shapes + [jax.ShapeDtypeStruct(fetch[0].shape[1:], fetch[0].dtype)]
        out_specs = out_specs + [vmem]
        scratch = scratch + [pltpu.SemaphoreType.DMA((fetch[0].shape[1],))]
    if weights is None:
        out_shapes[0] = pltpu.HBM(out_shapes[0].shape, out_shapes[0].dtype)
    made = pl.pallas_call(
        body,
        in_specs=in_specs,
        out_specs=out_specs,
        out_shape=out_shapes,
        scratch_shapes=scratch,
        compiler_params=params(8),
        cost_estimate=pl.CostEstimate(
            flops=3 * tests * depth * dim,
            bytes_accessed=2 * tests * dim,
            transcendentals=tests * depth,
        ),
        name=name,
    )(*operands)
    sq = made[1] if fresh else center_sq
    return made[0], sq, made[-1] if fetch is not None else None


def finished(kernels, weights, totals, places):
    blocks = places.shape[0]
    tests, depth = kernels[0].shape
    width = weights.shape[1]
    height = len(kernels) * tests // blocks
    unit = min(height, tests)

    def body(places_ref, *refs):
        kernel_refs, weight_ref = refs[: len(kernels)], refs[len(kernels)]
        total_refs, out_ref = refs[len(kernels) + 1 : -1], refs[-1]
        for start in range(0, blocks * height, unit):
            c, at = divmod(start, tests)
            block, within = divmod(start, height)
            value = jnp.dot(
                kernel_refs[c][at : at + unit, :], weight_ref[...], preferred_element_type=f32
            )
            value = value + total_refs[c][at : at + unit, :]
            out_ref[places_ref[block], within : within + unit, :] = value.astype(bf16)

    return pl.pallas_call(
        body,
        in_specs=[smem] + [vmem] * (len(kernels) + 1 + len(totals)),
        out_specs=vmem,
        out_shape=jax.ShapeDtypeStruct((blocks, height, width), bf16),
        compiler_params=params(8),
        cost_estimate=pl.CostEstimate(
            flops=4 * blocks * height * depth * width,
            bytes_accessed=2 * blocks * height * depth,
            transcendentals=0,
        ),
        name="finished",
    )(places, *kernels, weights, *totals)


class Piece:
    def __init__(self, cost, make, fetches=False):
        self.cost, self.make, self.done, self.fetches = cost, make, False, fetches

    def run(self, before, fetch=None):
        if not self.done:
            self.done = True
            return self.make(before, fetch) if fetch else self.make(before)


class Beside:
    def __init__(self):
        self.pieces = []
        self.wanted = None
        self.fetched = None

    def want(self, wanted):
        self.wanted, self.fetched = wanted, None

    def take(self):
        fetched, self.wanted, self.fetched = self.fetched, None, None
        return fetched

    def tie(self, before, received, room, fetch=False):
        while True:
            self.pieces = [p for p in self.pieces if not p.done]
            fitting = [p for p in self.pieces if p.cost <= 2 * room]
            if not fitting:
                return received
            piece = fitting[0]
            room -= piece.cost
            if fetch and self.wanted and piece.fetches:
                made = piece.run(before, self.wanted)
                self.wanted, self.fetched = None, made[-1]
                made = made[:-1]
            else:
                made = piece.run(before)
                made = made[:-1] if piece.fetches else made
            received, _ = lax.optimization_barrier((received, made))

    def rest(self):
        for piece in self.pieces:
            piece.run(None)


def after(value, before):
    if before is None:
        return value
    return lax.optimization_barrier((value, before))[0]


def swap(value, axis, mask):
    size = lax.axis_size(axis)
    return lax.ppermute(value, axis, [(i, i ^ mask) for i in range(size)])


def added(left, right):
    return left.astype(f32) + right.astype(f32)


def col_steps():
    bits = lax.axis_size("col").bit_length() - 1
    place = lax.axis_index("col")
    bit = [(place >> j) & 1 for j in range(bits)]
    masks = [1 << j for j in range(bits)]
    if bits >= 3:
        bit[bits - 2] = bit[bits - 2] ^ bit[bits - 1]
        masks[-1] += masks[-2]
    return masks, bit


def packed(bits):
    number = jnp.int32(0)
    for b in bits:
        number = number * 2 + b
    return number


def row_sum(partial, work):
    bits = lax.axis_size("row").bit_length() - 1
    parts = [partial[p] for p in range(partial.shape[0])]
    orders = [list(range(bits)), list(range(bits))[::-1]]
    for j in range(bits):
        received = [swap(p, "row", 1 << o[j]) for p, o in zip(parts, orders)]
        received = work.tie(parts, received, row_room, j == bits - 1)
        parts = [added(p, r) for p, r in zip(parts, received)]
        if j < bits - 1:
            parts = [p.astype(bf16) for p in parts]
    return jnp.concatenate(parts, axis=0)


def subtracted(own, total, work):
    masks, _ = col_steps()
    for j, mask in enumerate(masks[:-1]):
        half = total.shape[0] // 2
        mine, other = total[:half], total[half:]
        received = work.tie(other, swap(other, "col", mask), core_room if j == 0 else near_room)
        total = added(mine, received).astype(bf16)
    received = work.tie(total, swap(total, "col", masks[-1]), far_room)
    value = (own.astype(f32) - added(total, received)).astype(bf16)
    for j, mask in reversed(list(enumerate(masks[:-1]))):
        received = work.tie(
            value, swap(value, "col", mask), core_room if j == 0 else near_room, True
        )
        value = jnp.concatenate([value, received], axis=0)
    return value


def scattered(total):
    masks, _ = col_steps()
    for j, mask in enumerate(masks):
        half = total.shape[0] // 2
        total = added(total[:half], swap(total[half:], "col", mask))
        if j < len(masks) - 1:
            total = total.astype(bf16)
    return total[0]


def shards(factor_blocks, inverse_blocks, right_side, centers, owner_map, test_pool, test_rows):
    panels = inverse_blocks.shape[0]
    col_tiles = inverse_blocks.shape[1]
    tile_size = inverse_blocks.shape[2]
    row_tiles = inverse_blocks.shape[3]
    width_out = right_side.shape[3]
    own_rows = row_tiles * tile_size
    tests = test_rows.shape[0]
    chunks = 4
    chunk = tests // chunks
    group = chunks

    _, kept = col_steps()
    parts = 2 ** (len(kept) - 1)
    flip = packed(kept[:-1])
    flip_ref = flip.reshape(1)
    targets = right_side.reshape(panels, parts, own_rows // parts, width_out)
    size = 2 ** len(kept)
    blocks = np.arange(size)
    digits = [(blocks >> j) & 1 for j in range(len(kept))]
    if len(kept) >= 3:
        digits[-2] = digits[-2] ^ digits[-1]
    places = sum(d << (len(kept) - 1 - j) for j, d in enumerate(digits)).astype(np.int32)
    places = jnp.asarray(places) ^ packed(kept)

    work = Beside()
    span = [None] * chunks
    norms = [None] * chunks
    center_sq = [None] * panels
    first = [None] * chunks
    totals = [None] * chunks
    solved = [None] * panels
    rounded = [None] * panels
    partial = [None] * panels

    tiles = owner_map.shape[0]
    match = owner_map == jnp.arange(tiles, dtype=jnp.int32)[None, :]
    slots = jnp.sum(match * jnp.arange(tiles, dtype=jnp.int32)[:, None], axis=0)
    located = test_rows - lax.axis_index("row") * test_pool.shape[0]

    def gather(i, count):
        def make(before):
            made = gathered(
                after(located[i * chunk : (i + count) * chunk], before), test_pool, count, f"gathered_{i}"
            )
            span[i : i + count] = made[:count]
            norms[i : i + count] = made[count:]
            return made

        return Piece(min(1.3 + 2.6 * count, 6.0), make)

    def panel_slots(k, before):
        return after(slots[k * col_tiles : (k + 1) * col_tiles], before)

    def score(k, i):
        def make(before, fetch=None):
            made, center_sq[k], fetched = scored(
                span[i], norms[i], centers, center_sq[k], panel_slots(k, before),
                rounded[k] if k > 0 else None, totals[i] if k > 0 else None, fetch,
                f"scored_{k}_{i}",
            )
            if k > 0:
                totals[i] = made
            else:
                first[i] = made
            return made, fetched

        return Piece(2.5 if k > 0 else 2.7, make, True)

    def factor(early, k, kept=None):
        def make(before):
            partial[early] = panel_product(
                factor_blocks,
                pair_slot(early, k),
                kept,
                after(rounded[k], before)[None],
                None,
                partial[early],
                parts,
                flip_ref,
                bf16 if early == k - 1 else f32,
                f"factor_{early}_{k}",
            )
            return partial[early]

        return Piece(3.6, make)

    work.pieces += [gather(i, group) for i in range(0, chunks, group)]
    work.pieces += [score(0, i) for i in range(chunks)]
    ahead = []
    for k in range(panels - 1, -1, -1):
        if k == panels - 1:
            residue, residue_flip = targets[k], None
        else:
            for early, piece in ahead:
                if early == k:
                    piece.run(None)
            factor(k, k + 1, work.take()).run(None)
            if k > 0:
                work.want((inverse_blocks, k))
            own = lax.dynamic_slice(
                targets, (k, flip, 0, 0), (1, 1) + targets.shape[2:]
            )[0]
            residue, residue_flip = subtracted(own, partial[k], work), flip_ref
        product = panel_product(
            inverse_blocks, k, work.take(), residue, residue_flip, None, row_parts, None, bf16,
            f"inverse_{k}",
        )
        if k > 0:
            work.want((factor_blocks, pair_slot(k - 1, k)))
        solved[k] = row_sum(product, work)
        rounded[k] = solved[k].astype(bf16)
        early = [(e, factor(e, k)) for e in range(k - 2, -1, -1)]
        ahead += early
        if k > 0:
            early = [piece for _, piece in early]
            work.pieces[:0] = early[:1]
            work.pieces += early[1:] + [score(k, i) for i in range(chunks)]
    work.rest()
    estimate = scattered(finished(first, rounded[0], totals, places))
    alpha = jnp.stack(solved).reshape(panels, col_tiles, tile_size, width_out)
    return (alpha, estimate)


def solution(mesh):
    in_specs = (
        P(None, None, "row", None, "col"),
        P(None, None, "col", None, "row"),
        P(None, None, "row", None),
        P(None, "col", None),
        P(None, "col"),
        P("row", None),
        P("row"),
    )
    out_specs = (P(None, None, "col", None), P(("row", "col"), None))
    return jax.shard_map(shards, mesh=mesh, in_specs=in_specs, out_specs=out_specs, check_vma=False)
```
